32 devices in a mesh: row: 8 (over z, y), col: 4 (over x, core).
Axes of the slice: x: 2, y: 2, z: 4, core: 2. Of those that a mesh axis runs over, the one named last changes fastest.
Arguments:
- factor: float32 [8, 12, 1024, 4, 1024], P('row', None, None, None, 'col'), may hold values from -0.01953125 to 0.01953125
- knowns: float32 [8, 12, 1024, 256], P('row'), may hold values from -6 to 6
- inverse: float32 [4, 1024, 1024], P(None, None, 'col'), may hold values from -0.1875 to 0.1875
Outputs:
- solved: float32 [4, 1024, 256], P(None, 'col', 'row')
The draws below stay inside these ranges and needn't reach their ends.
All inputs are finite; a program needn't handle non-finite values.
Results may differ from the reference program's by a relative error of at most 0.0001.
Values sent between devices are 32-bit elements; how exact they have to be, the bound alone decides.
No kernel may reach another device: no remote copies, remote signals or barrier semaphores. Data moves between devices by JAX's collectives and lax.ppermute only.
A program may use at most 128 MiB of HBM per device.

```python
import jax
import jax.numpy as jnp
from jax import lax

NB = 1024
NBLK = 96
SRC = 256
KW = 4
ROWGRID = 8
BPR = 12
ORDER = 98304


def level_of(key, shape, shards, least, largest):
    level = 1.0
    for axis_at, blocks in shards:
        draws = jax.random.uniform(jax.random.fold_in(jax.random.fold_in(key, 6), axis_at), (blocks,), jnp.float32, least / len(shards), largest / len(shards))
        level = level * jnp.repeat(jnp.exp(draws), shape[axis_at] // blocks).reshape((-1,) + (1,) * (len(shape) - 1 - axis_at))
    return level


def noise(rng, shape, spread, most, split=(), kind=jnp.bfloat16):
    entries = spread * jax.random.normal(rng, shape, jnp.float32)
    if split:
        entries = entries * level_of(rng, shape, split, -0.22, 0.18)
    return jnp.clip(entries, -most, most).astype(kind)


def setup_inputs(seed: int = 0) -> dict:
    splits = jax.random.split(jax.random.key(seed), 4)
    factor = noise(splits[0], (ROWGRID, BPR, NB, KW, NB), ORDER ** -0.5, 0.01953125, ((0, 8), (4, 4)), jnp.float32)
    knowns = noise(splits[1], (ROWGRID, BPR, NB, SRC), 1.0, 6.0, ((0, 8),), jnp.float32)
    inverse = noise(splits[2], (KW, NB, NB), NB ** -0.5, 0.1875, ((2, 4),), jnp.float32)
    return dict(factor=factor, knowns=knowns, inverse=inverse)


def reference(factor, knowns, inverse):
    first_block = NBLK - KW
    blockid = jnp.arange(BPR, dtype=jnp.int32)[None, :] * ROWGRID + jnp.arange(ROWGRID, dtype=jnp.int32)[:, None]
    keep_mask = (blockid < first_block).astype(knowns.dtype)
    masked = knowns * keep_mask[:, :, None, None]

    def add_rows(running, pieces):
        piece_factor, piece_knowns = pieces
        return running + jnp.einsum("lajc,las->jcs", piece_factor, piece_knowns, precision=lax.Precision.HIGHEST), None

    prefix, _ = lax.scan(add_rows, jnp.zeros((KW, NB, SRC), knowns.dtype), (factor, masked))
    solved = []
    for step in range(KW):
        block_id = first_block + step
        residual = knowns[block_id % ROWGRID, block_id // ROWGRID] - prefix[step]
        for earlier in range(step):
            other = first_block + earlier
            rows_block = factor[other % ROWGRID, other // ROWGRID, :, step, :]
            residual = residual - jnp.dot(rows_block.T, solved[earlier], precision=lax.Precision.HIGHEST)
        solved.append(jnp.dot(inverse[step].T, residual, precision=lax.Precision.HIGHEST))
    return jnp.stack(solved)
```

```python
import functools

import jax
import jax.numpy as jnp
from jax import lax
from jax.experimental import pallas as pl
from jax.experimental.pallas import tpu as pltpu
from jax.sharding import PartitionSpec as P

F32 = jnp.float32
BF16 = jnp.bfloat16
LANES = 128


def split(value):
    high = value.astype(BF16)
    return high, (value - high.astype(F32)).astype(BF16)


def dot3(left, right):
    product = functools.partial(jnp.dot, preferred_element_type=F32)
    return product(left[0], right[0]) + (product(left[1], right[0]) + product(left[0], right[1]))


def swap_pairs(size, mask):
    return [(i, i ^ mask) for i in range(size)]


def factor_rows(factor):
    blocks, order, window, width = factor.shape
    tiles = width // LANES
    view = factor.reshape(blocks * order, window, tiles, LANES).transpose(0, 2, 1, 3)
    return view.reshape(blocks * order * tiles * window, LANES)


def prefix_kernel(dims, knowns_ref, factor_ref, send_first, keep_first, send_rest, keep_rest, total):
    rows, window, tiles, first_block, groups, part = dims
    step = pl.program_id(0)
    row = lax.axis_index("row")
    col = lax.axis_index("col")
    order, sources = knowns_ref.shape
    width = tiles * LANES
    stride = tiles * window

    @pl.when(step == 0)
    def _():
        total[...] = jnp.zeros_like(total)

    @pl.when(step * rows + row < first_block)
    def _():
        known = split(knowns_ref[...].T)
        for j in range(window):
            pieces = [
                split(factor_ref[pl.ds(t * window + j, order, stride=stride), :]) for t in range(tiles)
            ]
            high = jnp.concatenate([p[0] for p in pieces], axis=1)
            low = jnp.concatenate([p[1] for p in pieces], axis=1)
            total[j] += dot3(known, (high, low))

    @pl.when(step == pl.num_programs(0) - 1)
    def _():
        rhs = knowns_ref[pl.ds(pl.multiple_of(col * width, width), width), :].T
        bit = lax.rem(row, 2)
        for j in range(window):
            block_id = first_block + j
            own = (row == block_id % rows).astype(F32)
            total[j] = own * rhs - total[j]
        for j in range(window):
            keep, send = (keep_first, send_first) if j == 0 else (keep_rest, send_rest)
            at = 0 if j == 0 else j - 1
            for piece in range(groups * window // 2):
                mine = pl.multiple_of((2 * piece + bit) * part, part)
                other = pl.multiple_of((2 * piece + 1 - bit) * part, part)
                keep[at, piece] = total[j, pl.ds(mine, part), :]
                send[at, piece] = total[j, pl.ds(other, part), :]


def window_kernel(window, tiles, factor_ref, *outs):
    member = lax.rem(lax.axis_index("row"), window)
    order = outs[0].shape[0]
    for ahead, out in enumerate(outs, 1):
        j = jnp.minimum(member + ahead, window - 1)
        for t in range(tiles):
            out[:, t * LANES : (t + 1) * LANES] = factor_ref[
                pl.ds(t * window + j, order, stride=tiles * window), :
            ]


def apply_kernel(negate, parts_ref, matrix_ref, *rest):
    out = rest[-1]
    chunks, sources, width = parts_ref.shape
    left = split(jnp.concatenate([parts_ref[q] for q in range(chunks)], axis=1))
    product = dot3(left, split(matrix_ref[...]))
    out[...] = rest[0][...] - product if negate else product


def apply(parts, matrix, base=None):
    chunks, sources, width = parts.shape
    args = (parts, matrix) if base is None else (parts, matrix, base)
    cost = pl.CostEstimate(
        flops=6 * matrix.size * sources, bytes_accessed=4 * (matrix.size + parts.size), transcendentals=0
    )
    return pl.pallas_call(
        functools.partial(apply_kernel, base is not None),
        out_shape=jax.ShapeDtypeStruct((sources, matrix.shape[1]), F32),
        cost_estimate=cost,
    )(*args)


def gather_col(block, col):
    held = block[None]
    size = lax.axis_size("col")
    mask = 1
    while mask < size:
        other = lax.ppermute(held, "col", swap_pairs(size, mask))
        mine_first = (col & mask) == 0
        held = jnp.concatenate(
            [jnp.where(mine_first, held, other), jnp.where(mine_first, other, held)], axis=0
        )
        mask *= 2
    return held


def on_device(factor, knowns, inverse):
    rows = lax.axis_size("row")
    row = lax.axis_index("row")
    col = lax.axis_index("col")
    _, blocks, order, window, width = factor.shape
    sources = knowns.shape[-1]
    first_block = blocks * rows - window
    tiles = width // LANES
    groups = rows // window
    part = sources // rows
    solver = (first_block % rows) // window
    member = row % window
    slot = first_block // rows
    base_row = solver * window
    row_stride = tiles * window
    flat = factor_rows(factor[0])
    own_knowns = knowns[0]

    own = pl.pallas_call(
        functools.partial(window_kernel, window, tiles),
        grid=(1,),
        in_specs=[pl.BlockSpec((order * row_stride, LANES), lambda i: (slot, 0))],
        out_specs=[pl.BlockSpec((order, width), lambda i: (0, 0))] * (window - 1),
        out_shape=[jax.ShapeDtypeStruct((order, width), F32)] * (window - 1),
        compiler_params=pltpu.CompilerParams(vmem_limit_bytes=40 << 20),
    )(flat)

    def among(pairs, payload):
        return lax.ppermute(payload, "row", [(base_row + a, base_row + b) for a, b in pairs])

    near1 = among([(0, 1), (1, 0), (2, 3)], own[0])
    far1 = among([(0, 2), (1, 3), (2, 0)], own[0])

    half = groups * window // 2
    first_shape = jax.ShapeDtypeStruct((1, half, part, width), F32)
    rest_shape = jax.ShapeDtypeStruct((window - 1, half, part, width), F32)
    whole = lambda shape: pl.BlockSpec(shape.shape, lambda i: (0,) * 4)
    send0, keep0, send1, keep1 = pl.pallas_call(
        functools.partial(prefix_kernel, (rows, window, tiles, first_block, groups, part)),
        grid=(blocks,),
        in_specs=[
            pl.BlockSpec((order, sources), lambda i: (i, 0)),
            pl.BlockSpec((order * row_stride, LANES), lambda i: (i, 0)),
        ],
        out_specs=[whole(first_shape), whole(first_shape), whole(rest_shape), whole(rest_shape)],
        out_shape=[first_shape, first_shape, rest_shape, rest_shape],
        scratch_shapes=[pltpu.VMEM((window, sources, width), F32)],
        compiler_params=pltpu.CompilerParams(vmem_limit_bytes=40 << 20),
        cost_estimate=pl.CostEstimate(
            flops=6 * flat.size * sources, bytes_accessed=4 * (flat.size + own_knowns.size), transcendentals=0
        ),
    )(own_knowns.reshape(blocks * order, sources), flat)

    def reduce_rows(send, keep):
        total = keep + lax.ppermute(send, "row", swap_pairs(rows, 1))
        mask = 2
        while mask < window:
            total = total.reshape(total.shape[0], -1, 2, part, width)
            bit = (row // mask) % 2
            keep = jnp.where(bit == 0, total[:, :, 0], total[:, :, 1])
            send = jnp.where(bit == 0, total[:, :, 1], total[:, :, 0])
            total = keep + lax.ppermute(send, "row", swap_pairs(rows, mask))
            mask *= 2
        mask = 1
        while mask < groups:
            pairs = []
            for group in range(groups):
                apart = group ^ solver
                if apart & mask and not apart & (mask - 1):
                    pairs += [(group * window + k, (group ^ mask) * window + k) for k in range(window)]
            total = total + lax.ppermute(total, "row", pairs)
            mask *= 2
        return total.reshape(total.shape[0], groups * part, width)

    residual = [reduce_rows(send0, keep0)[0]]

    near2 = among([(0, 1), (1, 0), (2, 3), (3, 2)], jnp.where(member < 2, own[1], far1))
    far2 = among([(0, 2), (1, 3), (3, 1)], jnp.where(member < 2, own[1], near1))
    residual += list(reduce_rows(send1, keep1))

    near3 = among([(0, 1), (2, 3), (3, 2)], jnp.where(member == 0, own[2], far2))
    far3 = among([(0, 2)], own[2])
    top = order // 2
    near4 = among([(2, 3)], far3[:top])
    far4 = among([(1, 3)], near3[top:])
    last = jnp.concatenate([near4, far4], axis=0)

    def choose(*options):
        out = options[-1]
        for at in range(len(options) - 2, -1, -1):
            out = jnp.where(member == at, options[at], out)
        return out

    between = {
        (0, 1): choose(own[0], near1, far1, near2),
        (1, 2): choose(near1, own[0], near2, far1),
        (2, 3): choose(far1, far2, own[0], near1),
        (0, 2): choose(own[1], near2, far2, near3),
        (1, 3): choose(near2, own[1], near3, far2),
        (0, 3): choose(own[2], near3, far3, last),
    }

    solved = []
    for j in range(window):
        x = apply(gather_col(residual[j], col), inverse[j])
        solved.append(x)
        if j + 1 < window:
            full = gather_col(x, col)
            for k in range(j + 1, window):
                residual[k] = apply(full, between[j, k], residual[k])

    stacked = jnp.stack(solved).reshape(window, groups, part, width)
    result = stacked[:, solver]
    for group in range(groups):
        if group != solver:
            pairs = [(base_row + k, group * window + k) for k in range(window)]
            moved = lax.ppermute(stacked[:, group], "row", pairs)
            result = jnp.where(row // window == group, moved, result)
    return result.transpose(0, 2, 1)


def solution(mesh):
    return jax.shard_map(
        on_device,
        mesh=mesh,
        in_specs=(
            P("row", None, None, None, "col"),
            P("row", None, None, None),
            P(None, None, "col"),
        ),
        out_specs=P(None, "col", "row"),
        check_vma=False,
    )
```

```python
import functools

import jax
import jax.numpy as jnp
from jax import lax
from jax.experimental import pallas as pl
from jax.experimental.pallas import tpu as pltpu
from jax.sharding import PartitionSpec as P

F32 = jnp.float32
BF16 = jnp.bfloat16
LANES = 128


def split(value):
    high = value.astype(BF16)
    return high, (value - high.astype(F32)).astype(BF16)


def dot3(left, right):
    product = functools.partial(jnp.dot, preferred_element_type=F32)
    return product(left[0], right[0]) + (product(left[1], right[0]) + product(left[0], right[1]))


def swap_pairs(size, mask):
    return [(i, i ^ mask) for i in range(size)]


def factor_rows(factor):
    blocks, order, window, width = factor.shape
    tiles = width // LANES
    view = factor.reshape(blocks * order, window, tiles, LANES).transpose(0, 2, 1, 3)
    return view.reshape(blocks * order * tiles * window, LANES)


def accumulate(dims, block, knowns_ref, factor_ref, total):
    rows, window, tiles, first_block = dims
    order = knowns_ref.shape[0]
    stride = tiles * window

    @pl.when(block * rows + lax.axis_index("row") < first_block)
    def _():
        known = split(knowns_ref[...].T)
        for j in range(window):
            pieces = [
                split(factor_ref[pl.ds(t * window + j, order, stride=stride), :]) for t in range(tiles)
            ]
            high = jnp.concatenate([p[0] for p in pieces], axis=1)
            low = jnp.concatenate([p[1] for p in pieces], axis=1)
            total[j] += dot3(known, (high, low))


def prefix_kernel(dims, groups, part, knowns_ref, factor_ref, send_first, keep_first, send_rest, keep_rest, total):
    rows, window, tiles, first_block = dims
    step = pl.program_id(0)
    row = lax.axis_index("row")
    col = lax.axis_index("col")
    width = tiles * LANES

    @pl.when(step == 0)
    def _():
        total[...] = jnp.zeros_like(total)

    accumulate(dims, step, knowns_ref, factor_ref, total)

    @pl.when(step == pl.num_programs(0) - 1)
    def _():
        rhs = knowns_ref[pl.ds(pl.multiple_of(col * width, width), width), :].T
        bit = lax.rem(row, 2)
        for j in range(window):
            own = (row == (first_block + j) % rows).astype(F32)
            total[j] = own * rhs - total[j]
        for j in range(window):
            early = keep_first.shape[0]
            keep, send = (keep_first, send_first) if j < early else (keep_rest, send_rest)
            at = j if j < early else j - early
            for piece in range(groups * window // 2):
                mine = pl.multiple_of((2 * piece + bit) * part, part)
                other = pl.multiple_of((2 * piece + 1 - bit) * part, part)
                keep[at, piece] = total[j, pl.ds(mine, part), :]
                send[at, piece] = total[j, pl.ds(other, part), :]


def window_kernel(window, tiles, least, factor_ref, *outs):
    member = lax.rem(lax.axis_index("row"), window)
    order = outs[0].shape[0]
    for ahead, out in enumerate(outs, least):
        j = jnp.minimum(member + ahead, window - 1)
        for t in range(tiles):
            out[:, t * LANES : (t + 1) * LANES] = factor_ref[
                pl.ds(t * window + j, order, stride=tiles * window), :
            ]


def dot(left, right):
    return jnp.dot(left, right, precision=lax.Precision.HIGH, preferred_element_type=F32)


def gather_col(block):
    size = lax.axis_size("col")
    col = lax.axis_index("col")
    held, mask = block, 1
    while mask < size:
        other = lax.ppermute(held, "col", swap_pairs(size, mask))
        first = (col & mask) == 0
        held = jnp.concatenate([jnp.where(first, held, other), jnp.where(first, other, held)], axis=1)
        mask *= 2
    return held


def on_device(factor, knowns, inverse):
    rows = lax.axis_size("row")
    row = lax.axis_index("row")
    col = lax.axis_index("col")
    _, blocks, order, window, width = factor.shape
    sources = knowns.shape[-1]
    first_block = blocks * rows - window
    tiles = width // LANES
    groups = rows // window
    part = sources // rows
    solver = (first_block % rows) // window
    member = row % window
    slot = first_block // rows
    base_row = solver * window
    row_stride = tiles * window
    flat = factor_rows(factor[0])
    own_knowns = knowns[0]

    cuts = 4

    def window_blocks(count):
        return pl.pallas_call(
            functools.partial(window_kernel, window, tiles, 1),
            grid=(cuts,),
            in_specs=[pl.BlockSpec((order // cuts * row_stride, LANES), lambda i: (slot * cuts + i, 0))],
            out_specs=[pl.BlockSpec((order // cuts, width), lambda i: (i, 0))] * count,
            out_shape=[jax.ShapeDtypeStruct((order, width), F32)] * count,
            compiler_params=pltpu.CompilerParams(vmem_limit_bytes=40 << 20),
        )(flat)

    def among(pairs, payload):
        return lax.ppermute(payload, "row", [(base_row + a, base_row + b) for a, b in pairs])

    early = 1
    top = order // 2
    next_block, *far_blocks = window_blocks(window - 1)
    with jax.named_scope("next_blocks"):
        near = among([(0, 1), (1, 0), (2, 3)], next_block)
        far = among([(0, 2), (1, 3), (2, 0)], next_block)

    half = groups * window // 2
    first_shape = jax.ShapeDtypeStruct((early, half, part, width), F32)
    rest_shape = jax.ShapeDtypeStruct((window - early, half, part, width), F32)
    whole = lambda shape: pl.BlockSpec(shape.shape, lambda i: (0,) * len(shape.shape))
    send0, keep0, send1, keep1 = pl.pallas_call(
        functools.partial(prefix_kernel, (rows, window, tiles, first_block), groups, part),
        grid=(blocks,),
        in_specs=[
            pl.BlockSpec((order, sources), lambda i: (i, 0)),
            pl.BlockSpec((order * row_stride, LANES), lambda i: (i, 0)),
        ],
        out_specs=[whole(first_shape), whole(first_shape), whole(rest_shape), whole(rest_shape)],
        out_shape=[first_shape, first_shape, rest_shape, rest_shape],
        scratch_shapes=[pltpu.VMEM((window, sources, width), F32)],
        compiler_params=pltpu.CompilerParams(vmem_limit_bytes=48 << 20),
        cost_estimate=pl.CostEstimate(
            flops=6 * flat.size * sources, bytes_accessed=4 * (flat.size + own_knowns.size), transcendentals=0
        ),
    )(own_knowns.reshape(blocks * order, sources), flat)

    send0, keep0, send1, keep1, near, far = lax.optimization_barrier((send0, keep0, send1, keep1, near, far))
    with jax.named_scope("next_blocks_relay"):
        near2 = among([(0, 1), (2, 3), (3, 2)], far[:top])
        far2 = among([(0, 2), (1, 3), (3, 1)], near[top:])
    def reduce_rows(send, keep, beside=()):
        total = keep + lax.ppermute(send, "row", swap_pairs(rows, 1))
        mask = 2
        while mask < window:
            total = total.reshape(total.shape[0], -1, 2, part, width)
            bit = (row // mask) % 2
            keep = jnp.where(bit == 0, total[:, :, 0], total[:, :, 1])
            send = jnp.where(bit == 0, total[:, :, 1], total[:, :, 0])
            total = keep + lax.ppermute(send, "row", swap_pairs(rows, mask))
            mask *= 2
        mask = 1
        while mask < groups:
            pairs = []
            for group in range(groups):
                apart = group ^ solver
                if apart & mask and not apart & (mask - 1):
                    pairs += [(group * window + k, (group ^ mask) * window + k) for k in range(window)]
            moved, *beside = lax.optimization_barrier((lax.ppermute(total, "row", pairs), *beside))
            total = total + moved
            mask *= 2
        return total.reshape(total.shape[0], groups * part, width), beside

    with jax.named_scope("reduce_first"):
        first, (near2, far2) = reduce_rows(send0, keep0, (near2, far2))
    with jax.named_scope("reduce_rest"):
        rest, _ = reduce_rows(send1, keep1)
    residual = [*first, *rest]

    with jax.named_scope("pick"):
        third = jnp.concatenate([near2, far2])

        def pick(*options):
            out = options[-1]
            for place in range(window - 1):
                out = jnp.where(member == place, options[place], out)
            return out

        above = [
            pick(next_block, near, far, third),
            pick(near, next_block, third, far),
            pick(far, third, next_block, near),
        ]
    def far_terms(owner, x):
        others = [k for k in range(window) if k != owner]
        shares = jnp.concatenate([x] + [among([(k, owner)], x) for k in others])
        blocks_here = far_blocks[: window - 2 - owner]
        terms = dot(shares, jnp.concatenate(blocks_here, axis=1)).reshape(window, x.shape[0], -1)
        total = jnp.where(member == owner, terms[0], 0.0)
        for at, k in enumerate(others, 1):
            total = total + among([(owner, k)], terms[at])
        return [total[:, at * width : (at + 1) * width] for at in range(len(blocks_here))]

    solved = []
    for j in range(window):
        with jax.named_scope(f"solve{j}"):
            solved.append(dot(gather_col(residual[j]), inverse[j]))
            if j + 1 == window:
                break
            x = gather_col(solved[j])
        if j + 2 < window:
            with jax.named_scope(f"far{j}"):
                for k, term in enumerate(far_terms(j, x), j + 2):
                    residual[k] = residual[k] - term
        with jax.named_scope(f"next{j}"):
            residual[j + 1] = residual[j + 1] - dot(x, above[j])

    stacked = jnp.stack(solved).reshape(window, groups, part, width)
    result = stacked[:, solver]
    for group in range(groups):
        if group != solver:
            pairs = [(base_row + k, group * window + k) for k in range(window)]
            moved = lax.ppermute(stacked[:, group], "row", pairs)
            result = jnp.where(row // window == group, moved, result)
    return result.transpose(0, 2, 1)


def solution(mesh):
    return jax.shard_map(
        on_device,
        mesh=mesh,
        in_specs=(
            P("row", None, None, None, "col"),
            P("row", None, None, None),
            P(None, None, "col"),
        ),
        out_specs=P(None, "col", "row"),
        check_vma=False,
    )
```

```python
import functools

import jax
import jax.numpy as jnp
from jax import lax
from jax.experimental import pallas as pl
from jax.experimental.pallas import tpu as pltpu
from jax.sharding import PartitionSpec as P

F32 = jnp.float32
BF16 = jnp.bfloat16
LANES = 128


def split(value):
    high = value.astype(BF16)
    return high, (value - high.astype(F32)).astype(BF16)


def dot3(left, right):
    product = functools.partial(jnp.dot, preferred_element_type=F32)
    return product(left[0], right[0]) + (product(left[1], right[0]) + product(left[0], right[1]))


def swap_pairs(size, mask):
    return [(i, i ^ mask) for i in range(size)]


def factor_rows(factor):
    blocks, order, window, width = factor.shape
    tiles = width // LANES
    view = factor.reshape(blocks * order, window, tiles, LANES).transpose(0, 2, 1, 3)
    return view.reshape(blocks * order * tiles * window, LANES)


def accumulate(dims, block, knowns_ref, factor_ref, total):
    rows, window, tiles, first_block = dims
    order = knowns_ref.shape[0]
    stride = tiles * window

    @pl.when(block * rows + lax.axis_index("row") < first_block)
    def _():
        known = split(knowns_ref[...].T)
        for j in range(window):
            pieces = [
                split(factor_ref[pl.ds(t * window + j, order, stride=stride), :]) for t in range(tiles)
            ]
            high = jnp.concatenate([p[0] for p in pieces], axis=1)
            low = jnp.concatenate([p[1] for p in pieces], axis=1)
            total[j] += dot3(known, (high, low))


def prefix_kernel(dims, part, sizes, knowns_ref, factor_ref, *refs):
    keeps, sends, total = refs[: len(sizes)], refs[len(sizes) : -1], refs[-1]
    rows, window, tiles, first_block = dims
    step = pl.program_id(0)
    row = lax.axis_index("row")
    col = lax.axis_index("col")
    width = tiles * LANES

    @pl.when(step == 0)
    def _():
        total[...] = jnp.zeros_like(total)

    accumulate(dims, step, knowns_ref, factor_ref, total)

    @pl.when(step == pl.num_programs(0) - 1)
    def _():
        rhs = knowns_ref[pl.ds(pl.multiple_of(col * width, width), width), :].T
        bit = lax.rem(row, 2)
        j = 0
        for keep, send, size in zip(keeps, sends, sizes):
            for at in range(size):
                own = (row == (first_block + j) % rows).astype(F32)
                total[j] = own * rhs - total[j]
                for piece in range(rows // 2):
                    mine = pl.multiple_of((2 * piece + bit) * part, part)
                    other = pl.multiple_of((2 * piece + 1 - bit) * part, part)
                    keep[at, piece] = total[j, pl.ds(mine, part), :]
                    send[at, piece] = total[j, pl.ds(other, part), :]
                j += 1


def window_kernel(window, tiles, least, factor_ref, *outs):
    member = lax.rem(lax.axis_index("row"), window)
    order = outs[0].shape[0]
    for ahead, out in enumerate(outs, least):
        j = jnp.minimum(member + ahead, window - 1)
        for t in range(tiles):
            out[:, t * LANES : (t + 1) * LANES] = factor_ref[
                pl.ds(t * window + j, order, stride=tiles * window), :
            ]


def dot(left, right):
    return jnp.dot(left, right, precision=lax.Precision.HIGH, preferred_element_type=F32)


def wait(event, arrays):
    return lax.optimization_barrier((event, *arrays))[1:]


def line_steps(count, target):
    below, above, steps = list(range(target)), list(range(count - 1, target, -1)), []
    while below or above:
        moves, taken = [], False
        for side in (below, above):
            pairs = [(side[at], side[at + 1]) for at in range(0, len(side) - 1, 2)]
            left = [to for _, to in pairs]
            if len(side) % 2:
                if taken:
                    left.append(side[-1])
                else:
                    pairs.append((side[-1], target))
                    taken = True
            moves += pairs
            side[:] = left
        steps.append(moves)
    return steps


def gather_col(block):
    return lax.all_gather(block, "col", axis=1, tiled=True)


def on_device(factor, knowns, inverse):
    rows = lax.axis_size("row")
    row = lax.axis_index("row")
    _, blocks, order, window, width = factor.shape
    sources = knowns.shape[-1]
    first_block = blocks * rows - window
    tiles = width // LANES
    part = sources // rows
    pieces = rows // 2
    slot = first_block // rows
    base_row = first_block % rows
    leader = row % 2 == 0
    row_stride = tiles * window
    flat = pltpu.with_memory_space_constraint(factor_rows(factor[0]), pltpu.HBM)
    own_knowns = knowns[0]
    cuts = 4

    ahead = pl.pallas_call(
        functools.partial(window_kernel, window, tiles, 1),
        grid=(cuts,),
        in_specs=[pl.BlockSpec((order // cuts * row_stride, LANES), lambda i: (slot * cuts + i, 0))],
        out_specs=[pl.BlockSpec((order // cuts, width), lambda i: (i, 0))] * (window - 1),
        out_shape=[jax.ShapeDtypeStruct((order, width), F32)] * (window - 1),
        compiler_params=pltpu.CompilerParams(vmem_limit_bytes=40 << 20),
    )(flat)

    def among(pairs, payload):
        return lax.ppermute(payload, "row", [(base_row + a, base_row + b) for a, b in pairs])

    with jax.named_scope("near1"):
        near = [among([(0, 1), (1, 0), (2, 3)], ahead[0])]
    with jax.named_scope("far"):
        far = among([(2, 0)], ahead[0])

    sizes = (1, 1, window - 2)
    shapes = [jax.ShapeDtypeStruct((size, pieces, part, width), F32) for size in sizes] * 2
    keeps_sends = pl.pallas_call(
        functools.partial(prefix_kernel, (rows, window, tiles, first_block), part, sizes),
        grid=(blocks,),
        in_specs=[
            pl.BlockSpec((order, sources), lambda i: (i, 0)),
            pl.BlockSpec((order * row_stride, LANES), lambda i: (i, 0)),
        ],
        out_specs=[pl.BlockSpec(shape.shape, lambda i: (0, 0, 0, 0)) for shape in shapes],
        out_shape=shapes,
        scratch_shapes=[pltpu.VMEM((window, sources, width), F32)],
        compiler_params=pltpu.CompilerParams(vmem_limit_bytes=48 << 20),
        cost_estimate=pl.CostEstimate(
            flops=6 * flat.size * sources, bytes_accessed=4 * (flat.size + own_knowns.size), transcendentals=0
        ),
    )(pltpu.with_memory_space_constraint(own_knowns.reshape(blocks * order, sources), pltpu.HBM), flat)
    keeps, sends = list(keeps_sends[: len(sizes)]), list(keeps_sends[len(sizes) :])
    sends[0], sends[1], near[0], far = lax.optimization_barrier((sends[0], sends[1], near[0], far))

    def reduce_rows(send, keep):
        total = keep + (yield lax.ppermute(send, "row", swap_pairs(rows, 1)))
        for moves in line_steps(pieces, base_row // 2):
            pairs = [(2 * a + k, 2 * b + k) for a, b in moves for k in (0, 1)]
            total = total + (yield lax.ppermute(total, "row", pairs))
        yield total.reshape(total.shape[0], pieces * part, width)

    with jax.named_scope("reduce0"):
        leading = reduce_rows(sends[0], keeps[0])
        lead = next(leading)
    with jax.named_scope("reduce1"):
        trailing = reduce_rows(*wait(lead, (sends[1],)), keeps[1])
        trail = next(trailing)
    with jax.named_scope("reduce2"):
        last = reduce_rows(*wait(trail, (sends[2],)), keeps[2])
        held = next(last)
    for step in range(len(line_steps(pieces, base_row // 2))):
        with jax.named_scope("reduce0"):
            lead = leading.send(lead)
        if step == 0:
            lead, trail = lax.optimization_barrier((lead, trail))
        else:
            lead, trail, held = lax.optimization_barrier((lead, trail, held))
        with jax.named_scope("reduce1"):
            trail = trailing.send(trail)
    after_first = wait(held, (near[0], *ahead[1:]))
    for _ in line_steps(pieces, base_row // 2):
        with jax.named_scope("reduce2"):
            held = last.send(held)
    residual = [one for gen, value in ((leading, lead), (trailing, trail), (last, held)) for one in gen.send(value)]

    def between(i, j):
        if i < 2:
            mine, other = ahead[j - i - 1], near[j - i - 1]
            return jnp.where(leader, mine, other) if i == 0 else jnp.where(leader, other, mine)
        return jnp.where(leader, far, across)

    with jax.named_scope("near2"):
        near.append(among([(0, 1), (1, 0)], after_first[1]))
    with jax.named_scope("near3"):
        near.append(among([(0, 1)], after_first[2]))
    with jax.named_scope("across"):
        across = among([(3, 1)], after_first[0])

    solved = []
    for j in range(window):
        with jax.named_scope(f"solve{j}"):
            full = gather_col(residual[j])
            solved.append(dot(full, inverse[j]))
            if j + 1 == window:
                break
            x = gather_col(solved[j])
        if j == 0:
            corner = x
        for k in range(j + 1, window):
            with jax.named_scope(f"term{j}{k}"):
                if (j, k) != (0, window - 1):
                    residual[k] = residual[k] - dot(x, between(j, k))
        if j == 2:
            with jax.named_scope("corner"):
                residual[window - 1] = residual[window - 1] - dot(corner, between(0, window - 1))

    def hand_out(values):
        parts = values.reshape(-1, pieces, part, width)
        home = base_row // 2
        result = jnp.where(row // 2 == home, parts[:, home], 0.0)
        for piece in range(pieces):
            if piece != home:
                pairs = [(base_row + k, 2 * piece + k) for k in (0, 1)]
                result = result + lax.ppermute(parts[:, piece], "row", pairs)
        return result

    with jax.named_scope("out"):
        result = hand_out(jnp.stack(solved))
    return result.transpose(0, 2, 1)


def solution(mesh):
    return jax.shard_map(
        on_device,
        mesh=mesh,
        in_specs=(
            P("row", None, None, None, "col"),
            P("row", None, None, None),
            P(None, None, "col"),
        ),
        out_specs=P(None, "col", "row"),
        check_vma=False,
    )
```

```python
import functools

import jax
import jax.numpy as jnp
from jax import lax
from jax.experimental import pallas as pl
from jax.experimental.pallas import tpu as pltpu
from jax.sharding import PartitionSpec as P

F32 = jnp.float32
BF16 = jnp.bfloat16
LANES = 128


def split(value):
    high = value.astype(BF16)
    return high, (value - high.astype(F32)).astype(BF16)


def dot3(left, right):
    product = functools.partial(jnp.dot, preferred_element_type=F32)
    return product(left[0], right[0]) + (product(left[1], right[0]) + product(left[0], right[1]))


def swap_pairs(size, mask):
    return [(i, i ^ mask) for i in range(size)]


def factor_rows(factor):
    blocks, order, window, width = factor.shape
    tiles = width // LANES
    view = factor.reshape(blocks * order, window, tiles, LANES).transpose(0, 2, 1, 3)
    return view.reshape(blocks * order, tiles * window, 1, LANES)


def prefix_kernel(dims, part, sizes, knowns_ref, *refs):
    rows, window, tiles, first_block, order = dims
    columns, refs = refs[: tiles * window], refs[tiles * window :]
    keeps, sends, total = refs[: len(sizes)], refs[len(sizes) : -1], refs[-1]
    step = pl.program_id(0)
    row = lax.axis_index("row")
    col = lax.axis_index("col")
    width = tiles * LANES
    depth = knowns_ref.shape[0]
    per_step = depth // order

    @pl.when(step == 0)
    def _():
        total[...] = jnp.zeros_like(total)

    counted = [
        knowns_ref[at * order : (at + 1) * order, :]
        * (((step * per_step + at) * rows + row) < first_block).astype(F32)
        for at in range(per_step)
    ]
    known = split(jnp.concatenate(counted, axis=0).T)
    for j in range(window):
        pieces = [split(columns[t * window + j].reshape(depth, LANES)[...]) for t in range(tiles)]
        high = jnp.concatenate([p[0] for p in pieces], axis=1)
        low = jnp.concatenate([p[1] for p in pieces], axis=1)
        total[j] += dot3(known, (high, low))

    @pl.when(step == pl.num_programs(0) - 1)
    def _():
        first_row = depth - order + col * width
        rhs = knowns_ref[pl.ds(pl.multiple_of(first_row, width), width), :].T
        bit = lax.rem(row, 2)
        j = 0
        for keep, send, size in zip(keeps, sends, sizes):
            for at in range(size):
                own = (row == (first_block + j) % rows).astype(F32)
                total[j] = own * rhs - total[j]
                for piece in range(rows // 2):
                    mine = pl.multiple_of((2 * piece + bit) * part, part)
                    other = pl.multiple_of((2 * piece + 1 - bit) * part, part)
                    keep[at, piece] = total[j, pl.ds(mine, part), :]
                    send[at, piece] = total[j, pl.ds(other, part), :]
                j += 1


def window_kernel(window, tiles, factor_ref, *outs):
    member = lax.rem(lax.axis_index("row"), window)
    order = outs[0].shape[0]
    for ahead, out in enumerate(outs, 1):
        j = jnp.minimum(member + ahead, window - 1)
        for t in range(tiles):
            out[:, t * LANES : (t + 1) * LANES] = factor_ref[
                pl.ds(t * window + j, order, stride=tiles * window), :
            ]


def dot(left, right):
    return jnp.dot(left, right, precision=lax.Precision.HIGH, preferred_element_type=F32)


def wait(event, arrays):
    return lax.optimization_barrier((event, *arrays))[1:]


def line_steps(count, target):
    below, above, steps = list(range(target)), list(range(count - 1, target, -1)), []
    while below or above:
        moves, taken = [], False
        for side in (below, above):
            pairs = [(side[at], side[at + 1]) for at in range(0, len(side) - 1, 2)]
            left = [to for _, to in pairs]
            if len(side) % 2:
                if taken:
                    left.append(side[-1])
                else:
                    pairs.append((side[-1], target))
                    taken = True
            moves += pairs
            side[:] = left
        steps.append(moves)
    return steps


def gather_col(block):
    return lax.all_gather(block, "col", axis=1, tiled=True)


def on_device(factor, knowns, inverse):
    rows = lax.axis_size("row")
    row = lax.axis_index("row")
    _, blocks, order, window, width = factor.shape
    sources = knowns.shape[-1]
    first_block = blocks * rows - window
    tiles = width // LANES
    part = sources // rows
    pieces = rows // 2
    slot = first_block // rows
    base_row = first_block % rows
    leader = row % 2 == 0
    columns = tiles * window
    view = factor_rows(factor[0])
    flat = pltpu.with_memory_space_constraint(view.reshape(-1, LANES), pltpu.HBM)
    view = pltpu.with_memory_space_constraint(view, pltpu.HBM)
    own_knowns = knowns[0]
    cuts = 4

    ahead = pl.pallas_call(
        functools.partial(window_kernel, window, tiles),
        grid=(cuts,),
        in_specs=[pl.BlockSpec((order // cuts * columns, LANES), lambda i: (slot * cuts + i, 0))],
        out_specs=[pl.BlockSpec((order // cuts, width), lambda i: (i, 0))] * (window - 1),
        out_shape=[jax.ShapeDtypeStruct((order, width), F32)] * (window - 1),
        compiler_params=pltpu.CompilerParams(vmem_limit_bytes=40 << 20),
    )(flat)

    def among(pairs, payload):
        return lax.ppermute(payload, "row", [(base_row + a, base_row + b) for a, b in pairs])

    with jax.named_scope("near1"):
        near = [among([(0, 1), (1, 0), (2, 3)], ahead[0])]
    with jax.named_scope("far"):
        far = among([(2, 0)], ahead[0])

    sizes = (1, window - 1)
    shapes = [(size, pieces, part, width) for size in sizes] * 2
    per_step = 2 if blocks % 2 == 0 else 1
    depth = per_step * order
    keeps_sends = pl.pallas_call(
        functools.partial(prefix_kernel, (rows, window, tiles, first_block, order), part, sizes),
        grid=(blocks // per_step,),
        in_specs=[pl.BlockSpec((depth, sources), lambda i: (i, 0))]
        + [
            pl.BlockSpec((depth, 1, 1, LANES), functools.partial(lambda at, i: (i, at, 0, 0), at))
            for at in range(columns)
        ],
        out_specs=[pl.BlockSpec(shape, lambda i: (0, 0, 0, 0)) for shape in shapes],
        out_shape=[pltpu.VMEM(shape, F32) for shape in shapes[: len(sizes)]]
        + [jax.ShapeDtypeStruct(shape, F32) for shape in shapes[len(sizes) :]],
        scratch_shapes=[pltpu.VMEM((window, sources, width), F32)],
        compiler_params=pltpu.CompilerParams(vmem_limit_bytes=52 << 20),
        cost_estimate=pl.CostEstimate(
            flops=6 * flat.size * sources, bytes_accessed=4 * (flat.size + own_knowns.size), transcendentals=0
        ),
    )(
        pltpu.with_memory_space_constraint(own_knowns.reshape(blocks * order, sources), pltpu.HBM),
        *[view] * columns,
    )
    keeps, sends = list(keeps_sends[: len(sizes)]), list(keeps_sends[len(sizes) :])
    sends[0], sends[1], near[0], far = lax.optimization_barrier((sends[0], sends[1], near[0], far))


    home = base_row // 2

    def moves_to(moves):
        return [(2 * a + k, 2 * b + k) for a, b in moves for k in (0, 1)]

    with jax.named_scope("reduce0"):
        arrived = lax.ppermute(sends[0], "row", swap_pairs(rows, 1))
        lead = keeps[0] + arrived
        places = [place for place in range(pieces) if place != home]
        straight = [lax.ppermute(lead, "row", moves_to([(place, home)])) for place in places]
    with jax.named_scope("reduce1"):
        trail_arrived = lax.ppermute(*wait(arrived, (sends[1],)), "row", swap_pairs(rows, 1))
    after_trail = wait(trail_arrived, (near[0], *ahead[1:]))
    with jax.named_scope("near2"):
        near.append(among([(0, 1), (1, 0)], after_trail[1]))
    *straight, trail_arrived = lax.optimization_barrier((*straight, trail_arrived))
    with jax.named_scope("reduce0"):
        for one in straight:
            lead = lead + one
    with jax.named_scope("reduce1"):
        trail = keeps[1] + trail_arrived
        for moves in line_steps(pieces, home):
            trail = trail + lax.ppermute(trail, "row", moves_to(moves))
    with jax.named_scope("across"):
        across = among([(3, 1)], *wait(trail, (near[0],)))
    with jax.named_scope("near3"):
        near.append(among([(0, 1)], after_trail[2]))
    residual = [one.reshape(pieces * part, width) for one in (*lead, *trail)]

    def between(i, j):
        if i < 2:
            mine, other = ahead[j - i - 1], near[j - i - 1]
            return jnp.where(leader, mine, other) if i == 0 else jnp.where(leader, other, mine)
        return jnp.where(leader, far, across)

    def hand_out(values):
        parts = values.reshape(-1, pieces, part, width)
        result = jnp.where(row // 2 == home, parts[:, home], 0.0)
        for piece in range(pieces):
            if piece != home:
                pairs = [(base_row + k, 2 * piece + k) for k in (0, 1)]
                result = result + lax.ppermute(parts[:, piece], "row", pairs)
        return result

    solved = []
    for j in range(window - 1):
        with jax.named_scope(f"solve{j}"):
            solved.append(dot(gather_col(residual[j]), inverse[j]))
            x = gather_col(solved[j])
        if j == 0:
            corner = x
        for k in range(j + 1, window):
            with jax.named_scope(f"term{j}{k}"):
                if (j, k) != (0, window - 1):
                    residual[k] = residual[k] - dot(x, between(j, k))
        if j == 2:
            with jax.named_scope("corner"):
                residual[window - 1] = residual[window - 1] - dot(corner, between(0, window - 1))
    with jax.named_scope("out_last"):
        own = hand_out(residual[-1])[0]
        own_solved = dot(gather_col(own), inverse[window - 1])
    with jax.named_scope("out"):
        result = jnp.concatenate([hand_out(jnp.stack(solved)), own_solved[None]])
    return result.transpose(0, 2, 1)


def solution(mesh):
    return jax.shard_map(
        on_device,
        mesh=mesh,
        in_specs=(
            P("row", None, None, None, "col"),
            P("row", None, None, None),
            P(None, None, "col"),
        ),
        out_specs=P(None, "col", "row"),
        check_vma=False,
    )
```

```python
import functools

import jax
import jax.numpy as jnp
from jax import lax
from jax.experimental import pallas as pl
from jax.experimental.pallas import tpu as pltpu
from jax.sharding import PartitionSpec as P

F32 = jnp.float32
BF16 = jnp.bfloat16
LANES = 128


def split(value):
    high = value.astype(BF16)
    return high, (value - high.astype(F32)).astype(BF16)


def dot3(left, right):
    product = functools.partial(jnp.dot, preferred_element_type=F32)
    return product(left[0], right[0]) + (product(left[1], right[0]) + product(left[0], right[1]))


def swap_pairs(size, mask):
    return [(i, i ^ mask) for i in range(size)]


def factor_rows(factor):
    blocks, order, window, width = factor.shape
    tiles = width // LANES
    view = factor.reshape(blocks * order, window, tiles, LANES).transpose(0, 2, 1, 3)
    return view.reshape(blocks * order, tiles * window, 1, LANES)


def prefix_kernel(dims, part, sizes, knowns_ref, *refs):
    rows, window, tiles, first_block, order = dims
    columns, refs = refs[: tiles * window], refs[tiles * window :]
    keeps, sends, total = refs[: len(sizes)], refs[len(sizes) : -1], refs[-1]
    step = pl.program_id(0)
    row = lax.axis_index("row")
    col = lax.axis_index("col")
    width = tiles * LANES
    depth = knowns_ref.shape[0]
    per_step = depth // order

    @pl.when(step == 0)
    def _():
        total[...] = jnp.zeros_like(total)

    counted = [
        knowns_ref[at * order : (at + 1) * order, :]
        * (((step * per_step + at) * rows + row) < first_block).astype(F32)
        for at in range(per_step)
    ]
    known = split(jnp.concatenate(counted, axis=0).T)
    for j in range(window):
        pieces = [split(columns[t * window + j].reshape(depth, LANES)[...]) for t in range(tiles)]
        high = jnp.concatenate([p[0] for p in pieces], axis=1)
        low = jnp.concatenate([p[1] for p in pieces], axis=1)
        total[j] += dot3(known, (high, low))

    @pl.when(step == pl.num_programs(0) - 1)
    def _():
        first_row = depth - order + col * width
        rhs = knowns_ref[pl.ds(pl.multiple_of(first_row, width), width), :].T
        bit = lax.rem(row, 2)
        j = 0
        for keep, send, size in zip(keeps, sends, sizes):
            for at in range(size):
                own = (row == (first_block + j) % rows).astype(F32)
                total[j] = own * rhs - total[j]
                for piece in range(rows // 2):
                    mine = pl.multiple_of((2 * piece + bit) * part, part)
                    other = pl.multiple_of((2 * piece + 1 - bit) * part, part)
                    keep[at, piece] = total[j, pl.ds(mine, part), :]
                    send[at, piece] = total[j, pl.ds(other, part), :]
                j += 1


def window_kernel(window, tiles, factor_ref, *outs):
    member = lax.rem(lax.axis_index("row"), window)
    order = outs[0].shape[0]
    for ahead, out in enumerate(outs, 1):
        j = jnp.minimum(member + ahead, window - 1)
        for t in range(tiles):
            out[:, t * LANES : (t + 1) * LANES] = factor_ref[
                pl.ds(t * window + j, order, stride=tiles * window), :
            ]


def dot(left, right):
    return jnp.dot(left, right, precision=lax.Precision.HIGH, preferred_element_type=F32)


def wait(event, arrays):
    return lax.optimization_barrier((event, *arrays))[1:]


def line_steps(count, target):
    below, above, steps = list(range(target)), list(range(count - 1, target, -1)), []
    while below or above:
        moves, taken = [], False
        for side in (below, above):
            pairs = [(side[at], side[at + 1]) for at in range(0, len(side) - 1, 2)]
            left = [to for _, to in pairs]
            if len(side) % 2:
                if taken:
                    left.append(side[-1])
                else:
                    pairs.append((side[-1], target))
                    taken = True
            moves += pairs
            side[:] = left
        steps.append(moves)
    return steps


def gather_col(block):
    return lax.all_gather(block, "col", axis=1, tiled=True)


def on_device(factor, knowns, inverse):
    rows = lax.axis_size("row")
    row = lax.axis_index("row")
    _, blocks, order, window, width = factor.shape
    sources = knowns.shape[-1]
    first_block = blocks * rows - window
    tiles = width // LANES
    part = sources // rows
    pieces = rows // 2
    slot = first_block // rows
    base_row = first_block % rows
    leader = row % 2 == 0
    columns = tiles * window
    view = factor_rows(factor[0])
    flat = pltpu.with_memory_space_constraint(view.reshape(-1, LANES), pltpu.HBM)
    view = pltpu.with_memory_space_constraint(view, pltpu.HBM)
    own_knowns = knowns[0]
    cuts = 4

    ahead = pl.pallas_call(
        functools.partial(window_kernel, window, tiles),
        grid=(cuts,),
        in_specs=[pl.BlockSpec((order // cuts * columns, LANES), lambda i: (slot * cuts + i, 0))],
        out_specs=[pl.BlockSpec((order // cuts, width), lambda i: (i, 0))] * (window - 1),
        out_shape=[jax.ShapeDtypeStruct((order, width), F32)] * (window - 1),
        compiler_params=pltpu.CompilerParams(vmem_limit_bytes=40 << 20),
    )(flat)

    def among(pairs, payload):
        return lax.ppermute(payload, "row", [(base_row + a, base_row + b) for a, b in pairs])

    with jax.named_scope("near1"):
        near = [among([(0, 1), (1, 0), (2, 3)], ahead[0])]
    with jax.named_scope("far"):
        far = among([(2, 0)], ahead[0])

    sizes = (1, window - 1)
    shapes = [(size, pieces, part, width) for size in sizes] * 2
    per_step = 2 if blocks % 2 == 0 else 1
    depth = per_step * order
    keeps_sends = pl.pallas_call(
        functools.partial(prefix_kernel, (rows, window, tiles, first_block, order), part, sizes),
        grid=(blocks // per_step,),
        in_specs=[pl.BlockSpec((depth, sources), lambda i: (i, 0))]
        + [
            pl.BlockSpec((depth, 1, 1, LANES), functools.partial(lambda at, i: (i, at, 0, 0), at))
            for at in range(columns)
        ],
        out_specs=[pl.BlockSpec(shape, lambda i: (0, 0, 0, 0)) for shape in shapes],
        out_shape=[pltpu.VMEM(shape, F32) for shape in shapes[: len(sizes)]]
        + [jax.ShapeDtypeStruct(shape, F32) for shape in shapes[len(sizes) :]],
        scratch_shapes=[pltpu.VMEM((window, sources, width), F32)],
        compiler_params=pltpu.CompilerParams(vmem_limit_bytes=52 << 20),
        cost_estimate=pl.CostEstimate(
            flops=6 * flat.size * sources, bytes_accessed=4 * (flat.size + own_knowns.size), transcendentals=0
        ),
    )(
        pltpu.with_memory_space_constraint(own_knowns.reshape(blocks * order, sources), pltpu.HBM),
        *[view] * columns,
    )
    keeps, sends = list(keeps_sends[: len(sizes)]), list(keeps_sends[len(sizes) :])
    sends[0], sends[1], near[0], far = lax.optimization_barrier((sends[0], sends[1], near[0], far))


    home = base_row // 2

    def moves_to(moves):
        return [(2 * a + k, 2 * b + k) for a, b in moves for k in (0, 1)]

    def bring_home(values, places):
        return [lax.ppermute(values, "row", moves_to([(place, home)])) for place in places if place != home]

    with jax.named_scope("reduce0"):
        arrived = lax.ppermute(sends[0], "row", swap_pairs(rows, 1))
        lead = keeps[0] + arrived
        lead_shares = bring_home(lead, range(pieces))
    with jax.named_scope("reduce1"):
        trail_arrived = lax.ppermute(*wait(arrived, (sends[1],)), "row", swap_pairs(rows, 1))
    after_lead = wait(lead, ahead[1:])
    *lead_shares, trail_arrived = lax.optimization_barrier((*lead_shares, trail_arrived))
    with jax.named_scope("reduce0"):
        lead = sum(lead_shares, lead)
    with jax.named_scope("reduce1"):
        trail = keeps[1] + trail_arrived
        trail = sum(bring_home(trail, range(pieces)[::-1]), trail)
    with jax.named_scope("near2"):
        near.append(among([(0, 1), (1, 0)], after_lead[0]))
    with jax.named_scope("near3"):
        near.append(among([(0, 1)], after_lead[1]))
    with jax.named_scope("across"):
        across = among([(3, 1)], *wait(trail, (near[0],)))
    residual = [one.reshape(pieces * part, width) for one in (*lead, *trail)]

    def between(i, j):
        if i < 2:
            mine, other = ahead[j - i - 1], near[j - i - 1]
            return jnp.where(leader, mine, other) if i == 0 else jnp.where(leader, other, mine)
        return jnp.where(leader, far, across)

    def hand_out(values):
        parts = values.reshape(-1, pieces, part, width)
        result = jnp.where(row // 2 == home, parts[:, home], 0.0)
        for piece in sorted(range(pieces), key=lambda place: abs(place - home)):
            if piece != home:
                pairs = [(base_row + k, 2 * piece + k) for k in (0, 1)]
                result = result + lax.ppermute(parts[:, piece], "row", pairs)
        return result

    solved = []
    for j in range(window - 1):
        with jax.named_scope(f"solve{j}"):
            solved.append(dot(gather_col(residual[j]), inverse[j]))
            x = gather_col(solved[j])
        if j == 0:
            corner = x
        for k in range(j + 1, window):
            with jax.named_scope(f"term{j}{k}"):
                if (j, k) != (0, window - 1):
                    residual[k] = residual[k] - dot(x, between(j, k))
        if j == 2:
            with jax.named_scope("corner"):
                residual[window - 1] = residual[window - 1] - dot(corner, between(0, window - 1))
    with jax.named_scope("out_last"):
        own = hand_out(residual[-1])[0]
        own_solved = dot(gather_col(own), inverse[window - 1])
    with jax.named_scope("out"):
        rest = hand_out(*wait(residual[-1], (jnp.stack(solved),)))
        result = jnp.concatenate([rest, own_solved[None]])
    return result.transpose(0, 2, 1)


def solution(mesh):
    return jax.shard_map(
        on_device,
        mesh=mesh,
        in_specs=(
            P("row", None, None, None, "col"),
            P("row", None, None, None),
            P(None, None, "col"),
        ),
        out_specs=P(None, "col", "row"),
        check_vma=False,
    )
```

```python
import functools

import jax
import jax.numpy as jnp
from jax import lax
from jax.experimental import pallas as pl
from jax.experimental.pallas import tpu as pltpu
from jax.sharding import PartitionSpec as P

F32 = jnp.float32
BF16 = jnp.bfloat16
LANES = 128


def split(value):
    high = value.astype(BF16)
    return high, (value - high.astype(F32)).astype(BF16)


def dot3(left, right):
    product = functools.partial(jnp.dot, preferred_element_type=F32)
    return product(left[0], right[0]) + (product(left[1], right[0]) + product(left[0], right[1]))


def swap_pairs(size, mask):
    return [(i, i ^ mask) for i in range(size)]


def factor_rows(factor):
    blocks, order, window, width = factor.shape
    tiles = width // LANES
    view = factor.reshape(blocks * order, window, tiles, LANES).transpose(0, 2, 1, 3)
    return view.reshape(blocks * order, tiles * window, 1, LANES)


def prefix_kernel(dims, part, sizes, knowns_ref, *refs):
    rows, window, tiles, first_block, order = dims
    columns, refs = refs[: tiles * window], refs[tiles * window :]
    keeps, sends, total = refs[: len(sizes)], refs[len(sizes) : -1], refs[-1]
    step = pl.program_id(0)
    row = lax.axis_index("row")
    col = lax.axis_index("col")
    width = tiles * LANES
    depth = knowns_ref.shape[0]
    per_step = depth // order

    @pl.when(step == 0)
    def _():
        total[...] = jnp.zeros_like(total)

    counted = [
        knowns_ref[at * order : (at + 1) * order, :]
        * (((step * per_step + at) * rows + row) < first_block).astype(F32)
        for at in range(per_step)
    ]
    known = split(jnp.concatenate(counted, axis=0).T)
    for j in range(window):
        pieces = [split(columns[t * window + j].reshape(depth, LANES)[...]) for t in range(tiles)]
        high = jnp.concatenate([p[0] for p in pieces], axis=1)
        low = jnp.concatenate([p[1] for p in pieces], axis=1)
        total[j] += dot3(known, (high, low))

    @pl.when(step == pl.num_programs(0) - 1)
    def _():
        first_row = depth - order + col * width
        rhs = knowns_ref[pl.ds(pl.multiple_of(first_row, width), width), :].T
        bit = lax.rem(row, 2)
        j = 0
        for keep, send, size in zip(keeps, sends, sizes):
            for at in range(size):
                own = (row == (first_block + j) % rows).astype(F32)
                total[j] = own * rhs - total[j]
                for piece in range(rows // 2):
                    mine = pl.multiple_of((2 * piece + bit) * part, part)
                    other = pl.multiple_of((2 * piece + 1 - bit) * part, part)
                    keep[at, piece] = total[j, pl.ds(mine, part), :]
                    send[at, piece] = total[j, pl.ds(other, part), :]
                j += 1


def window_kernel(window, tiles, factor_ref, *outs):
    member = lax.rem(lax.axis_index("row"), window)
    order = outs[0].shape[0]
    for ahead, out in enumerate(outs, 1):
        j = jnp.minimum(member + ahead, window - 1)
        for t in range(tiles):
            out[:, t * LANES : (t + 1) * LANES] = factor_ref[
                pl.ds(t * window + j, order, stride=tiles * window), :
            ]


def dot(left, right):
    return jnp.dot(left, right, precision=lax.Precision.HIGH, preferred_element_type=F32)


def wait(event, arrays):
    return lax.optimization_barrier((event, *arrays))[1:]


def line_steps(count, target):
    below, above, steps = list(range(target)), list(range(count - 1, target, -1)), []
    while below or above:
        moves, taken = [], False
        for side in (below, above):
            pairs = [(side[at], side[at + 1]) for at in range(0, len(side) - 1, 2)]
            left = [to for _, to in pairs]
            if len(side) % 2:
                if taken:
                    left.append(side[-1])
                else:
                    pairs.append((side[-1], target))
                    taken = True
            moves += pairs
            side[:] = left
        steps.append(moves)
    return steps


def gather_col(block):
    return lax.all_gather(block, "col", axis=1, tiled=True)


def on_device(factor, knowns, inverse):
    rows = lax.axis_size("row")
    row = lax.axis_index("row")
    _, blocks, order, window, width = factor.shape
    sources = knowns.shape[-1]
    first_block = blocks * rows - window
    tiles = width // LANES
    part = sources // rows
    pieces = rows // 2
    slot = first_block // rows
    base_row = first_block % rows
    leader = row % 2 == 0
    columns = tiles * window
    view = factor_rows(factor[0])
    flat = pltpu.with_memory_space_constraint(view.reshape(-1, LANES), pltpu.HBM)
    view = pltpu.with_memory_space_constraint(view, pltpu.HBM)
    own_knowns = knowns[0]
    cuts = 4

    ahead = pl.pallas_call(
        functools.partial(window_kernel, window, tiles),
        grid=(cuts,),
        in_specs=[pl.BlockSpec((order // cuts * columns, LANES), lambda i: (slot * cuts + i, 0))],
        out_specs=[pl.BlockSpec((order // cuts, width), lambda i: (i, 0))] * (window - 1),
        out_shape=[jax.ShapeDtypeStruct((order, width), F32)] * (window - 1),
        compiler_params=pltpu.CompilerParams(vmem_limit_bytes=40 << 20),
    )(flat)

    def among(pairs, payload):
        return lax.ppermute(payload, "row", [(base_row + a, base_row + b) for a, b in pairs])

    with jax.named_scope("near1"):
        near = [among([(0, 1), (1, 0), (2, 3)], ahead[0])]
    with jax.named_scope("far"):
        far = among([(2, 0)], ahead[0])

    sizes = (1, 1, window - 2)
    shapes = [(size, pieces, part, width) for size in sizes] * 2
    per_step = 2 if blocks % 2 == 0 else 1
    depth = per_step * order
    keeps_sends = pl.pallas_call(
        functools.partial(prefix_kernel, (rows, window, tiles, first_block, order), part, sizes),
        grid=(blocks // per_step,),
        in_specs=[pl.BlockSpec((depth, sources), lambda i: (i, 0))]
        + [
            pl.BlockSpec((depth, 1, 1, LANES), functools.partial(lambda at, i: (i, at, 0, 0), at))
            for at in range(columns)
        ],
        out_specs=[pl.BlockSpec(shape, lambda i: (0, 0, 0, 0)) for shape in shapes],
        out_shape=[pltpu.VMEM(shape, F32) for shape in shapes[: len(sizes)]]
        + [jax.ShapeDtypeStruct(shape, F32) for shape in shapes[len(sizes) :]],
        scratch_shapes=[pltpu.VMEM((window, sources, width), F32)],
        compiler_params=pltpu.CompilerParams(vmem_limit_bytes=52 << 20),
        cost_estimate=pl.CostEstimate(
            flops=6 * flat.size * sources, bytes_accessed=4 * (flat.size + own_knowns.size), transcendentals=0
        ),
    )(
        pltpu.with_memory_space_constraint(own_knowns.reshape(blocks * order, sources), pltpu.HBM),
        *[view] * columns,
    )
    keeps, sends = list(keeps_sends[: len(sizes)]), list(keeps_sends[len(sizes) :])
    sends[0], sends[1], near[0], far = lax.optimization_barrier((sends[0], sends[1], near[0], far))


    home = base_row // 2

    def moves_to(moves):
        return [(2 * a + k, 2 * b + k) for a, b in moves for k in (0, 1)]

    steps = [moves_to(moves) for moves in line_steps(pieces, home)]
    with jax.named_scope("reduce0"):
        arrived = lax.ppermute(sends[0], "row", swap_pairs(rows, 1))
        lead = keeps[0] + arrived
        places = [place for place in range(pieces) if place != home]
        lead_shares = [lax.ppermute(lead, "row", moves_to([(place, home)])) for place in places]
    after_arrival = wait(arrived, sends[1:])
    after_lead = wait(lead, ahead[1:])
    with jax.named_scope("reduce1"):
        second = keeps[1] + lax.ppermute(after_arrival[0], "row", swap_pairs(rows, 1))
        for pairs in steps:
            second = second + lax.ppermute(second, "row", pairs)
    with jax.named_scope("reduce2"):
        others = keeps[2] + lax.ppermute(after_arrival[1], "row", swap_pairs(rows, 1))
        others_arrived = lax.ppermute(others, "row", steps[0])
    with jax.named_scope("near2"):
        near.append(among([(0, 1), (1, 0)], after_lead[0]))
    with jax.named_scope("near3"):
        near.append(among([(0, 1)], after_lead[1]))
    with jax.named_scope("reduce0"):
        lead = sum(lead_shares, lead)
    residual = [one.reshape(pieces * part, width) for one in (*lead, *second)]

    def between(i, j):
        if i < 2:
            mine, other = ahead[j - i - 1], near[j - i - 1]
            return jnp.where(leader, mine, other) if i == 0 else jnp.where(leader, other, mine)
        return jnp.where(leader, far, across)

    def hand_out(values):
        parts = values.reshape(-1, pieces, part, width)
        result = jnp.where(row // 2 == home, parts[:, home], 0.0)
        for piece in sorted(range(pieces), key=lambda place: -abs(place - home)):
            if piece != home:
                pairs = [(base_row + k, 2 * piece + k) for k in (0, 1)]
                result = result + lax.ppermute(parts[:, piece], "row", pairs)
        return result

    solved = []
    for j in range(window - 1):
        with jax.named_scope(f"solve{j}"):
            solved.append(dot(gather_col(residual[j]), inverse[j]))
            x = gather_col(solved[j])
        if j == 0:
            with jax.named_scope("reduce2"):
                x, others_arrived = lax.optimization_barrier((x, others_arrived))
                others = others + others_arrived
            with jax.named_scope("across"):
                across = among([(3, 1)], *wait(others, (near[0],)))
            with jax.named_scope("reduce2"):
                for pairs in steps[1:]:
                    others = others + lax.ppermute(others, "row", pairs)
            residual += [one.reshape(pieces * part, width) for one in others]
            corner = x
        for k in range(j + 1, window):
            with jax.named_scope(f"term{j}{k}"):
                if (j, k) != (0, window - 1):
                    residual[k] = residual[k] - dot(x, between(j, k))
        if j == 2:
            with jax.named_scope("corner"):
                residual[window - 1] = residual[window - 1] - dot(corner, between(0, window - 1))
    with jax.named_scope("out_last"):
        own = hand_out(residual[-1])[0]
        own_solved = dot(gather_col(own), inverse[window - 1])
    with jax.named_scope("out"):
        rest = hand_out(*wait(residual[-1], (jnp.stack(solved),)))
        result = jnp.concatenate([rest, own_solved[None]])
    return result.transpose(0, 2, 1)


def solution(mesh):
    return jax.shard_map(
        on_device,
        mesh=mesh,
        in_specs=(
            P("row", None, None, None, "col"),
            P("row", None, None, None),
            P(None, None, "col"),
        ),
        out_specs=P(None, "col", "row"),
        check_vma=False,
    )
```

```python
import functools

import jax
import jax.numpy as jnp
from jax import lax
from jax.experimental import pallas as pl
from jax.experimental.pallas import tpu as pltpu
from jax.sharding import PartitionSpec as P

F32 = jnp.float32
BF16 = jnp.bfloat16
LANES = 128


def split(value):
    high = value.astype(BF16)
    return high, (value - high.astype(F32)).astype(BF16)


def dot3(left, right):
    product = functools.partial(jnp.dot, preferred_element_type=F32)
    return product(left[0], right[0]) + (product(left[1], right[0]) + product(left[0], right[1]))


def swap_pairs(size, mask):
    return [(i, i ^ mask) for i in range(size)]


def factor_rows(factor):
    blocks, order, window, width = factor.shape
    tiles = width // LANES
    view = factor.reshape(blocks * order, window, tiles, LANES).transpose(0, 2, 1, 3)
    return view.reshape(blocks * order, tiles * window, 1, LANES)


def prefix_kernel(dims, part, sizes, knowns_ref, *refs):
    rows, window, tiles, first_block, order = dims
    columns, refs = refs[: tiles * window], refs[tiles * window :]
    keeps, sends, total = refs[: len(sizes)], refs[len(sizes) : -1], refs[-1]
    step = pl.program_id(0)
    row = lax.axis_index("row")
    col = lax.axis_index("col")
    width = tiles * LANES
    depth = knowns_ref.shape[0]
    per_step = depth // order

    @pl.when(step == 0)
    def _():
        total[...] = jnp.zeros_like(total)

    counted = [
        knowns_ref[at * order : (at + 1) * order, :]
        * (((step * per_step + at) * rows + row) < first_block).astype(F32)
        for at in range(per_step)
    ]
    known = split(jnp.concatenate(counted, axis=0).T)
    for j in range(window):
        pieces = [split(columns[t * window + j].reshape(depth, LANES)[...]) for t in range(tiles)]
        high = jnp.concatenate([p[0] for p in pieces], axis=1)
        low = jnp.concatenate([p[1] for p in pieces], axis=1)
        total[j] += dot3(known, (high, low))

    @pl.when(step == pl.num_programs(0) - 1)
    def _():
        first_row = depth - order + col * width
        rhs = knowns_ref[pl.ds(pl.multiple_of(first_row, width), width), :].T
        bit = lax.rem(row, 2)
        j = 0
        for keep, send, size in zip(keeps, sends, sizes):
            for at in range(size):
                own = (row == (first_block + j) % rows).astype(F32)
                total[j] = own * rhs - total[j]
                for piece in range(rows // 2):
                    mine = pl.multiple_of((2 * piece + bit) * part, part)
                    other = pl.multiple_of((2 * piece + 1 - bit) * part, part)
                    keep[at, piece] = total[j, pl.ds(mine, part), :]
                    send[at, piece] = total[j, pl.ds(other, part), :]
                j += 1


def window_kernel(window, tiles, factor_ref, *outs):
    member = lax.rem(lax.axis_index("row"), window)
    order = outs[0].shape[0]
    for ahead, out in enumerate(outs, 1):
        j = jnp.minimum(member + ahead, window - 1)
        for t in range(tiles):
            out[:, t * LANES : (t + 1) * LANES] = factor_ref[
                pl.ds(t * window + j, order, stride=tiles * window), :
            ]


def dot(left, right):
    return jnp.dot(left, right, precision=lax.Precision.HIGH, preferred_element_type=F32)


def wait(event, arrays):
    return lax.optimization_barrier((event, *arrays))[1:]


def line_steps(count, target):
    below, above, steps = list(range(target)), list(range(count - 1, target, -1)), []
    while below or above:
        moves, taken = [], False
        for side in (below, above):
            pairs = [(side[at], side[at + 1]) for at in range(0, len(side) - 1, 2)]
            left = [to for _, to in pairs]
            if len(side) % 2:
                if taken:
                    left.append(side[-1])
                else:
                    pairs.append((side[-1], target))
                    taken = True
            moves += pairs
            side[:] = left
        steps.append(moves)
    return steps


def gather_col(block):
    return lax.all_gather(block, "col", axis=1, tiled=True)


def on_device(factor, knowns, inverse):
    rows = lax.axis_size("row")
    row = lax.axis_index("row")
    _, blocks, order, window, width = factor.shape
    sources = knowns.shape[-1]
    first_block = blocks * rows - window
    tiles = width // LANES
    part = sources // rows
    pieces = rows // 2
    slot = first_block // rows
    base_row = first_block % rows
    leader = row % 2 == 0
    columns = tiles * window
    view = factor_rows(factor[0])
    flat = pltpu.with_memory_space_constraint(view.reshape(-1, LANES), pltpu.HBM)
    view = pltpu.with_memory_space_constraint(view, pltpu.HBM)
    own_knowns = knowns[0]
    cuts = 4

    ahead = pl.pallas_call(
        functools.partial(window_kernel, window, tiles),
        grid=(cuts,),
        in_specs=[pl.BlockSpec((order // cuts * columns, LANES), lambda i: (slot * cuts + i, 0))],
        out_specs=[pl.BlockSpec((order // cuts, width), lambda i: (i, 0))] * (window - 1),
        out_shape=[jax.ShapeDtypeStruct((order, width), F32)] * (window - 1),
        compiler_params=pltpu.CompilerParams(vmem_limit_bytes=40 << 20),
    )(flat)

    def among(pairs, payload):
        return lax.ppermute(payload, "row", [(base_row + a, base_row + b) for a, b in pairs])

    with jax.named_scope("near1"):
        near = [among([(0, 1), (1, 0), (2, 3)], ahead[0])]
    with jax.named_scope("far"):
        far = among([(2, 0)], ahead[0])

    sizes = (1, 1, window - 2)
    shapes = [(size, pieces, part, width) for size in sizes] * 2
    per_step = 2 if blocks % 2 == 0 else 1
    depth = per_step * order
    keeps_sends = pl.pallas_call(
        functools.partial(prefix_kernel, (rows, window, tiles, first_block, order), part, sizes),
        grid=(blocks // per_step,),
        in_specs=[pl.BlockSpec((depth, sources), lambda i: (i, 0))]
        + [
            pl.BlockSpec((depth, 1, 1, LANES), functools.partial(lambda at, i: (i, at, 0, 0), at))
            for at in range(columns)
        ],
        out_specs=[pl.BlockSpec(shape, lambda i: (0, 0, 0, 0)) for shape in shapes],
        out_shape=[pltpu.VMEM(shape, F32) for shape in shapes[: len(sizes)]]
        + [jax.ShapeDtypeStruct(shape, F32) for shape in shapes[len(sizes) :]],
        scratch_shapes=[pltpu.VMEM((window, sources, width), F32)],
        compiler_params=pltpu.CompilerParams(vmem_limit_bytes=52 << 20),
        cost_estimate=pl.CostEstimate(
            flops=6 * flat.size * sources, bytes_accessed=4 * (flat.size + own_knowns.size), transcendentals=0
        ),
    )(
        pltpu.with_memory_space_constraint(own_knowns.reshape(blocks * order, sources), pltpu.HBM),
        *[view] * columns,
    )
    keeps, sends = list(keeps_sends[: len(sizes)]), list(keeps_sends[len(sizes) :])
    sends[0], sends[1], near[0], far = lax.optimization_barrier((sends[0], sends[1], near[0], far))


    home = base_row // 2

    def moves_to(moves):
        return [(2 * a + k, 2 * b + k) for a, b in moves for k in (0, 1)]

    steps = [moves_to(moves) for moves in line_steps(pieces, home)]
    with jax.named_scope("reduce0"):
        arrived = lax.ppermute(sends[0], "row", swap_pairs(rows, 1))
        lead = keeps[0] + arrived
        places = [place for place in range(pieces) if place != home]
        lead_shares = [lax.ppermute(lead, "row", moves_to([(place, home)])) for place in places]
    after_arrival = wait(arrived, sends[1:])
    after_lead = wait(lead, ahead[1:])
    with jax.named_scope("reduce1"):
        second = keeps[1] + lax.ppermute(after_arrival[0], "row", swap_pairs(rows, 1))
        for pairs in steps:
            second = second + lax.ppermute(second, "row", pairs)
    with jax.named_scope("reduce2"):
        others = keeps[2] + lax.ppermute(after_arrival[1], "row", swap_pairs(rows, 1))
        others_arrived = lax.ppermute(others, "row", steps[0])
    with jax.named_scope("near2"):
        near.append(among([(0, 1), (1, 0)], after_lead[0]))
    with jax.named_scope("near3"):
        near.append(among([(0, 1)], after_lead[1]))
    with jax.named_scope("reduce0"):
        lead = sum(lead_shares, lead)
    residual = [one.reshape(pieces * part, width) for one in (*lead, *second)]

    def between(i, j):
        if i < 2:
            mine, other = ahead[j - i - 1], near[j - i - 1]
            return jnp.where(leader, mine, other) if i == 0 else jnp.where(leader, other, mine)
        return jnp.where(leader, far, across)

    solved = []
    for j in range(window - 1):
        with jax.named_scope(f"solve{j}"):
            solved.append(dot(gather_col(residual[j]), inverse[j]))
            x = gather_col(solved[j])
        if j == 0:
            with jax.named_scope("reduce2"):
                x, others_arrived = lax.optimization_barrier((x, others_arrived))
                others = others + others_arrived
            with jax.named_scope("across"):
                across = among([(3, 1)], *wait(others, (near[0],)))
            with jax.named_scope("reduce2"):
                for pairs in steps[1:]:
                    others = others + lax.ppermute(others, "row", pairs)
            residual += [one.reshape(pieces * part, width) for one in others]
            corner = x
        for k in range(j + 1, window):
            with jax.named_scope(f"term{j}{k}"):
                if (j, k) != (0, window - 1):
                    residual[k] = residual[k] - dot(x, between(j, k))
        if j == 2:
            with jax.named_scope("corner"):
                residual[window - 1] = residual[window - 1] - dot(corner, between(0, window - 1))
    with jax.named_scope("out"):
        last = residual[-1].reshape(pieces, part, width)
        rest = wait(residual[-1], (jnp.stack(solved),))[0].reshape(-1, pieces, part, width)
        own_last = jnp.where(row // 2 == home, last[home], 0.0)
        own_rest = jnp.where(row // 2 == home, rest[:, home], 0.0)
        for place in range(pieces):
            pairs = [(base_row + k, 2 * place + k) for k in (0, 1)]
            if place < home:
                own_last = own_last + lax.ppermute(last[place], "row", pairs)
                own_rest = own_rest + lax.ppermute(rest[:, place], "row", pairs)
            elif place > home:
                moved = lax.ppermute(jnp.concatenate([rest[:, place], last[place][None]]), "row", pairs)
                own_rest, own_last = own_rest + moved[:-1], own_last + moved[-1]
        own_solved = dot(gather_col(own_last), inverse[window - 1])
        result = jnp.concatenate([own_rest, own_solved[None]])
    return result.transpose(0, 2, 1)


def solution(mesh):
    return jax.shard_map(
        on_device,
        mesh=mesh,
        in_specs=(
            P("row", None, None, None, "col"),
            P("row", None, None, None),
            P(None, None, "col"),
        ),
        out_specs=P(None, "col", "row"),
        check_vma=False,
    )
```
